256 devices in a mesh: row: 16 (over x, y_lo, core), col: 16 (over z, y_hi).
Axes of the slice: x: 4, y: 4 (y_hi: 2, y_lo: 2; y = y_hi * 2 + y_lo), z: 8, core: 2. Of those that a mesh axis runs over, the one named last changes fastest.
Arguments:
- inputs: bfloat16 [2048, 12288], P('row', 'col'), may hold values from -6 to 6
- w_up: bfloat16 [12288, 12288], P('col', 'row'), may hold values from -0.0546875 to 0.0546875
- w_down: bfloat16 [12288, 12288], P('row', 'col'), may hold values from -0.0546875 to 0.0546875
- upstream: bfloat16 [2048, 12288], P('row', 'col'), may hold values from -6 to 6
Outputs:
- grad_input: bfloat16 [2048, 12288], P('row', 'col')
- grad_up: bfloat16 [12288, 12288], P('col', 'row')
- grad_down: bfloat16 [12288, 12288], P('row', 'col')
The draws below stay inside these ranges and needn't reach their ends.
All inputs are finite; a program needn't handle non-finite values.
Results may differ from the reference program's by a relative error of at most 0.034.
Values may be sent and summed in bfloat16 or wider, within the bound.
A program may use at most 64 MiB of HBM per device.

```python
import math
import jax
import jax.numpy as jnp
from jax import lax

D = 12288
FF = 12288
TOKENS = 2048
N_ROW = 16
N_COL = 16


def raised(array, rng, source, target, parts, factor):
    def block_of(position):
        return (jnp.arange(array.shape[position]) // (array.shape[position] // parts)).reshape((-1,) + (1,) * (array.ndim - 1 - position))

    first = jax.random.permutation(rng, parts)[block_of(target)]
    second = (block_of(target) + parts // 2) % parts
    return jnp.where((block_of(source) == first) | (block_of(source) == second), factor * array, array)


def block_scale(key, extent, cuts, least, high):
    loudness = 1.0
    for axis_at, blocks in cuts:
        heights = jax.random.uniform(jax.random.fold_in(jax.random.fold_in(key, 6), axis_at), (blocks,), jnp.float32, least / len(cuts), high / len(cuts))
        loudness = loudness * jnp.repeat(jnp.exp(heights), extent[axis_at] // blocks).reshape((-1,) + (1,) * (len(extent) - 1 - axis_at))
    return loudness


def noise(stream_key, extent, scale, reach, cuts=(), dtype=jnp.bfloat16):
    factor_of = block_scale(stream_key, extent, cuts, -0.22, 0.18) if cuts else 1.0
    result = jax.random.normal(stream_key, extent, jnp.float32) * scale * factor_of
    return jnp.minimum(jnp.maximum(result, -reach), reach).astype(dtype)


def bell_draw_with(stream_key, extent, spread, limit, split, heavy, dtype=jnp.bfloat16):
    values = spread * jax.random.normal(stream_key, extent, jnp.float32)
    if split:
        values = values * block_scale(stream_key, extent, split, -0.22, 0.18)
    return jnp.clip(raised(values, jax.random.fold_in(stream_key, 3), *heavy), -limit, limit).astype(dtype)


def setup_inputs(seed: int = 0) -> dict:
    splits = jax.random.split(jax.random.key(seed), 5)
    return {
        "inputs": bell_draw_with(splits[0], (TOKENS, D), 1.0, 6.0, ((0, 16), (1, 16)), (1, 0, 16, 2.0)),
        "w_up": noise(splits[1], (D, FF), D ** -0.5, 0.0546875, ((0, 16), (1, 16))),
        "w_down": noise(splits[2], (FF, D), FF ** -0.5, 0.0546875, ((0, 16), (1, 16))),
        "upstream": bell_draw_with(splits[3], (TOKENS, D), 1.0, 6.0, ((0, 16), (1, 16)), (1, 0, 16, 2.0)),
    }


def gelu_parts(preact):
    coeff = math.sqrt(2.0 / math.pi)
    cubic = 0.044715
    inner = coeff * (preact + cubic * preact * preact * preact)
    tangent = jnp.tanh(inner)
    value = 0.5 * preact * (1.0 + tangent)
    slope = 0.5 * (1.0 + tangent) + 0.5 * preact * (1.0 - tangent * tangent) * coeff * (1.0 + 3.0 * cubic * preact * preact)
    return (value, slope)

def round_sum(left, right, blocks):
    rows_count = left.shape[0]
    inner_count = left.shape[1]
    cols_count = right.shape[1]
    width = inner_count // blocks
    left_blocks = left.reshape(rows_count, blocks, width).transpose(1, 0, 2)
    right_blocks = right.reshape(blocks, width, cols_count)

    def step(total, pair):
        term = jnp.dot(pair[0], pair[1], preferred_element_type=jnp.float32)
        term = lax.optimization_barrier(term.astype(jnp.bfloat16))
        return (total + term.astype(jnp.float32), None)
    total, unused = lax.scan(step, jnp.zeros((rows_count, cols_count), jnp.float32), (left_blocks, right_blocks))
    return total

def reference(inputs, w_up, w_down, upstream):
    preact = round_sum(inputs, w_up, N_COL)
    activation, slope = gelu_parts(preact)
    act_low = activation.astype(jnp.bfloat16)
    grad_act = round_sum(upstream, w_down.T, N_COL)
    grad_pre = (grad_act * slope).astype(jnp.bfloat16)
    grad_input = round_sum(grad_pre, w_up.T, N_ROW).astype(jnp.bfloat16)
    factor = 1.0 / math.sqrt(TOKENS)
    grad_up = (jnp.dot(inputs.T, grad_pre, preferred_element_type=jnp.float32) * factor).astype(jnp.bfloat16)
    grad_down = (jnp.dot(act_low.T, upstream, preferred_element_type=jnp.float32) * factor).astype(jnp.bfloat16)
    return (grad_input, grad_up, grad_down)
```

```python
import functools
import math

import jax
import jax.numpy as jnp
from jax import lax
from jax.experimental import pallas as pl
from jax.experimental.pallas import tpu as pltpu
from jax.sharding import PartitionSpec as P

MESH = pl.DeviceIdType.MESH
BF = jnp.bfloat16
F32 = jnp.float32
RING = 8
HALF = 64
ORDER = (0, 2, 1, 3)


def mod8(value):
    return lax.rem(value + 64, 8)


def gelu_parts(preact):
    coeff = math.sqrt(2.0 / math.pi)
    cubic = 0.044715
    inner = coeff * (preact + cubic * preact * preact * preact)
    tangent = jnp.tanh(inner)
    value = 0.5 * preact * (1.0 + tangent)
    slope = 0.5 * (1.0 + tangent) + 0.5 * preact * (1.0 - tangent * tangent) * coeff * (
        1.0 + 3.0 * cubic * preact * preact
    )
    return (value, slope)


def dot(left, right, left_dim, right_dim):
    return lax.dot_general(
        left, right, (((left_dim,), (right_dim,)), ((), ())), preferred_element_type=F32
    )


def kernel(
    x_ref, wu_ref, wd_ref, g_ref,
    gi_ref, gu_ref, gd_ref,
    gath, part, rs_out, rs_in, fin, y_out, y_in, slope_ref, ag, acc_up, acc_down,
    gi_keep, gi_sib_out, gi_sib_in, gi_out, gi_in,
    gath_ss, gath_rs, sib_ss, sib_rs, rs_ss, rs_rs, y_ss, y_rs, agy_ss, agy_rs, ag_ss, ag_rs,
    gs_ss, gs_rs, gi_ss, gi_rs,
):
    r, c = lax.axis_index("row"), lax.axis_index("col")
    o, p = lax.div(r, 2), lax.rem(r, 2)
    z, yh = lax.div(c, 2), lax.rem(c, 2)
    sign = 1 - 2 * p
    up = (r, lax.rem(c + 2, 16))
    down = (r, lax.rem(c + 14, 16))
    partner = (r, c + 1 - 2 * yh)
    sibling = (r + 1 - 2 * p, c)

    def peer(index):
        return (2 * index + p, c)

    def remote(src, dst, send, recv, device):
        return pltpu.make_async_remote_copy(
            src_ref=src, dst_ref=dst, send_sem=send, recv_sem=recv,
            device_id=device, device_id_type=MESH,
        )

    barrier = pltpu.get_barrier_semaphore()
    for device in (up, down, partner, sibling):
        pl.semaphore_signal(barrier, inc=1, device_id=device, device_id_type=MESH)
    for k in range(1, 8):
        pl.semaphore_signal(
            barrier, inc=1, device_id=peer(mod8(o + k)), device_id_type=MESH
        )
    pl.semaphore_wait(barrier, 11)

    def block_of(s, direction):
        if direction == 0:
            return 2 * mod8(o + z - 1 - s)
        return 2 * mod8(o + z + 1 + s) + 1

    def zed(s, direction):
        return mod8(z - 1 - s) if direction == 0 else mod8(z + 1 + s)

    def gather_copy(a, s):
        to = mod8(o - z + sign * (1 + s))
        own = x_ref if a == 0 else g_ref
        return to, remote(
            own, gath.at[a, r], gath_ss.at[a, s], gath_rs.at[a, o], peer(to)
        )

    for a in range(2):
        for s in range(8):
            to, copy = gather_copy(a, s)

            @pl.when(to != o)
            def _(copy=copy):
                copy.start()

    gath[0, r] = x_ref[...]
    gath[1, r] = g_ref[...]

    def direct_index(s):
        return mod8(o + z - sign * (1 + s))

    def forward(a, s):
        source = direct_index(s)
        block = 2 * source + p

        @pl.when(source != o)
        def _():
            remote(
                gath.at[a, block], gath.at[a, block], gath_ss.at[a, 0],
                gath_rs.at[a, source], sibling,
            ).wait_recv()

        remote(
            gath.at[a, block], gath.at[a, block], sib_ss.at[a, s], sib_rs.at[a, s], sibling
        ).start()

    def sibling_wait(a, s):
        block = 2 * mod8(o + z + sign * (1 + s)) + 1 - p
        remote(
            gath.at[a, block], gath.at[a, block], sib_ss.at[a, s], sib_rs.at[a, s], sibling
        ).wait_recv()

    def pair(a, s):
        return jnp.concatenate(
            [gath[a, block_of(s, 0)], gath[a, block_of(s, 1)]], axis=0
        )

    def ring_copy(a, s, q):
        return remote(
            rs_out.at[a, s, q], rs_in.at[a, s, q], rs_ss.at[a, s, q], rs_rs.at[a, s, q],
            up if q < 2 else down,
        )

    def partial(a, s):
        if a == 0:
            return dot(pair(0, s), wu_ref[...], 1, 0)
        return dot(pair(1, s), wd_ref[...], 1, 1)

    def reduce_step(a, s):
        sibling_wait(a, s)
        part[...] = partial(a, s)

        @pl.when(s < 7)
        def _():
            forward(a, s + 1)

        for q in ORDER:
            rows = pl.ds(q * HALF, HALF)

            @pl.when(s == 0)
            def _():
                rs_out[a, 0, q] = part[rows, :].astype(BF)

            @pl.when(s > 0)
            def _():
                ring_copy(a, s - 1, q).wait_recv()
                total = part[rows, :] + rs_in[a, s - 1, q].astype(F32)

                @pl.when(s < 7)
                def _():
                    rs_out[a, s, q] = total.astype(BF)

                @pl.when(s == 7)
                def _():
                    fin[a, rows, :] = total
                    y_out[a, rows, :] = total.astype(BF)

            @pl.when(s < 7)
            def _():
                ring_copy(a, s, q).start()

    def y_copy(a):
        return remote(
            y_out.at[a, pl.ds((1 - yh) * 128, 128)], y_in.at[a], y_ss.at[a], y_rs.at[a], partner
        )

    def reduced(a):
        y_copy(a).wait_recv()
        return fin[a, pl.ds(yh * 128, 128), :] + y_in[a].astype(F32)

    def agy_copy(a):
        return remote(ag.at[a, z, yh], ag.at[a, z, yh], agy_ss.at[a], agy_rs.at[a], partner)

    def agy_wait(a):
        remote(
            ag.at[a, z, 1 - yh], ag.at[a, z, 1 - yh], agy_ss.at[a], agy_rs.at[a], partner
        ).wait_recv()

    def ag_first(a, direction):
        for half in range(2):
            piece = ag.at[a, z, direction, pl.ds(half * HALF, HALF)]
            q = 2 * direction + half
            remote(
                piece, piece, ag_ss.at[a, 0, q], ag_rs.at[a, 0, q],
                (r, lax.rem(c + 2 + 12 * direction, 16)),
            ).start()

    def ag_piece(a, s, q):
        direction, half = q // 2, q % 2
        return ag.at[a, zed(s, direction), direction, pl.ds(half * HALF, HALF)]

    def ag_step(a, s):
        for q in ORDER:
            piece = ag_piece(a, s, q)
            device = up if q < 2 else down
            remote(piece, piece, ag_ss.at[a, s, q], ag_rs.at[a, s, q], device).wait_recv()

            @pl.when(s < 6)
            def _():
                remote(
                    piece, piece, ag_ss.at[a, s + 1, q], ag_rs.at[a, s + 1, q], device
                ).start()

    def gathered(a, s):
        return jnp.concatenate([ag[a, zed(s, 0), 0], ag[a, zed(s, 1), 1]], axis=0)

    def accumulate(acc, left, right, first):
        for m in range(3):
            rows = pl.ds(m * 256, 256)
            term = dot(left[:, m * 256 : (m + 1) * 256], right, 0, 0)
            if first:
                acc[rows, :] = term
            else:
                acc[rows, :] += term

    def gi_dest(s):
        return mod8(o + z - sign * (1 + s))

    def gi_sib_copy(s):
        return remote(
            gi_sib_out.at[s], gi_sib_in.at[s], gs_ss.at[s], gs_rs.at[s], sibling
        )

    def gi_copy(s):
        return remote(
            gi_out.at[s], gi_in.at[o], gi_ss.at[s], gi_rs.at[o], peer(gi_dest(s))
        )

    def gi_start(s, rows_in):
        part[...] = dot(rows_in, wu_ref[...], 1, 1)
        gi_sib_out[s] = part[pl.ds((1 - p) * 128, 128), :].astype(BF)
        gi_sib_copy(s).start()
        gi_keep[s] = part[pl.ds(p * 128, 128), :]

    def gi_finish(s):
        gi_sib_copy(s).wait_recv()
        total = (gi_keep[s] + gi_sib_in[s].astype(F32)).astype(BF)
        dest = gi_dest(s)

        @pl.when(dest == o)
        def _():
            gi_in[o] = total

        @pl.when(dest != o)
        def _():
            gi_out[s] = total
            gi_copy(s).start()

    forward(0, 0)

    @pl.loop(0, 8)
    def _(s):
        reduce_step(0, s)

    y_copy(0).start()
    forward(1, 0)

    @pl.loop(0, 8)
    def _(s):
        reduce_step(1, s)

        @pl.when(s == 1)
        def _():
            value, slope = gelu_parts(reduced(0))
            slope_ref[...] = slope
            ag[0, z, yh] = value.astype(BF)
            agy_copy(0).start()

    y_copy(1).start()
    ag_first(0, yh)
    agy_wait(0)
    ag_first(0, 1 - yh)
    accumulate(acc_down, gathered(0, 7), pair(1, 7), True)

    @pl.loop(0, 7)
    def _(s):
        ag_step(0, s)

        @pl.when(s == 1)
        def _():
            ag[1, z, yh] = (reduced(1) * slope_ref[...]).astype(BF)
            agy_copy(1).start()

        accumulate(acc_down, gathered(0, s), pair(1, s), False)

    ag_first(1, yh)
    agy_wait(1)
    ag_first(1, 1 - yh)
    own_pre = gathered(1, 7)
    gi_start(7, own_pre)
    accumulate(acc_up, pair(0, 7), own_pre, True)
    gi_finish(7)
    factor = 1.0 / math.sqrt(2048)
    gd_ref[...] = (acc_down[...] * factor).astype(BF)

    @pl.loop(0, 7)
    def _(s):
        ag_step(1, s)
        pre = gathered(1, s)
        gi_start(s, pre)
        accumulate(acc_up, pair(0, s), pre, False)
        gi_finish(s)

    gu_ref[...] = (acc_up[...] * factor).astype(BF)

    total = gi_in[o].astype(F32)
    for k in range(1, 8):
        source = mod8(o + k)
        remote(
            gi_out.at[0], gi_in.at[source], gi_ss.at[0], gi_rs.at[source], sibling
        ).wait_recv()
        total += gi_in[source].astype(F32)
    gi_ref[...] = total.astype(BF)

    for a in range(2):
        y_copy(a).wait_send()
        agy_copy(a).wait_send()

        @pl.loop(0, 8)
        def _(s):
            to, copy = gather_copy(a, s)

            @pl.when(to != o)
            def _():
                copy.wait_send()

            remote(
                gath.at[a, 0], gath.at[a, 0], sib_ss.at[a, s], sib_rs.at[a, s], sibling
            ).wait_send()

        @pl.loop(0, 7)
        def _(s):
            for q in range(4):
                ring_copy(a, s, q).wait_send()
                piece = ag.at[a, 0, 0, pl.ds(0, HALF)]
                remote(
                    piece, piece, ag_ss.at[a, s, q], ag_rs.at[a, s, q], up
                ).wait_send()

    @pl.loop(0, 8)
    def _(s):
        gi_sib_copy(s).wait_send()

        @pl.when(gi_dest(s) != o)
        def _():
            gi_copy(s).wait_send()


def on_device(inputs, w_up, w_down, upstream):
    tokens, width = inputs.shape
    hidden = w_up.shape[1]
    dma = pltpu.SemaphoreType.DMA
    vmem = pl.BlockSpec(memory_space=pltpu.VMEM)
    return pl.pallas_call(
        kernel,
        out_shape=(
            jax.ShapeDtypeStruct((tokens, width), BF),
            jax.ShapeDtypeStruct((width, hidden), BF),
            jax.ShapeDtypeStruct((hidden, width), BF),
        ),
        in_specs=[vmem] * 4,
        out_specs=(vmem, vmem, vmem),
        scratch_shapes=[
            pltpu.VMEM((2, 16, 128, 768), BF),
            pltpu.VMEM((256, 768), F32),
            pltpu.VMEM((2, 7, 4, HALF, 768), BF),
            pltpu.VMEM((2, 7, 4, HALF, 768), BF),
            pltpu.VMEM((2, 256, 768), F32),
            pltpu.VMEM((2, 256, 768), BF),
            pltpu.VMEM((2, 128, 768), BF),
            pltpu.VMEM((128, 768), F32),
            pltpu.VMEM((2, 8, 2, 128, 768), BF),
            pltpu.VMEM((768, 768), F32),
            pltpu.VMEM((768, 768), F32),
            pltpu.VMEM((8, 128, 768), F32),
            pltpu.VMEM((8, 128, 768), BF),
            pltpu.VMEM((8, 128, 768), BF),
            pltpu.VMEM((8, 128, 768), BF),
            pltpu.VMEM((8, 128, 768), BF),
            dma((2, 8)), dma((2, 8)), dma((2, 8)), dma((2, 8)),
            dma((2, 7, 4)), dma((2, 7, 4)),
            dma((2,)), dma((2,)), dma((2,)), dma((2,)),
            dma((2, 7, 4)), dma((2, 7, 4)),
            dma((8,)), dma((8,)), dma((8,)), dma((8,)),
        ],
        compiler_params=pltpu.CompilerParams(
            collective_id=0, has_side_effects=True, vmem_limit_bytes=58 << 20
        ),
        cost_estimate=pl.CostEstimate(
            flops=5 * 2 * 2048 * 768 * 768, bytes_accessed=6 << 20, transcendentals=128 * 768
        ),
        name="block_backward",
    )(inputs, w_up, w_down, upstream)


def solution(mesh):
    in_specs = (P("row", "col"), P("col", "row"), P("row", "col"), P("row", "col"))
    out_specs = (P("row", "col"), P("col", "row"), P("row", "col"))
    return jax.shard_map(
        on_device, mesh=mesh, in_specs=in_specs, out_specs=out_specs, check_vma=False
    )
```

```python
import functools
import math

import jax
import jax.numpy as jnp
from jax import lax
from jax.experimental import pallas as pl
from jax.experimental.pallas import tpu as pltpu
from jax.sharding import PartitionSpec as P

MESH = pl.DeviceIdType.MESH
BF = jnp.bfloat16
F32 = jnp.float32
RING = 8
HALF = 64
REL = (4, 3, -3, 2, -2, 1, -1, 0)
PARTS = tuple((j, h) for j in range(2) for h in range(2))


def mod8(value):
    return lax.rem(value + 64, 8)


def gelu_parts(preact):
    coeff = math.sqrt(2.0 / math.pi)
    cubic = 0.044715
    inner = coeff * (preact + cubic * preact * preact * preact)
    tangent = jnp.tanh(inner)
    value = 0.5 * preact * (1.0 + tangent)
    slope = 0.5 * (1.0 + tangent) + 0.5 * preact * (1.0 - tangent * tangent) * coeff * (
        1.0 + 3.0 * cubic * preact * preact
    )
    return (value, slope)


def dot(left, right, left_dim, right_dim):
    return lax.dot_general(
        left, right, (((left_dim,), (right_dim,)), ((), ())), preferred_element_type=F32
    )


def kernel(
    x_ref, wu_ref, wd_ref, g_ref,
    gi_ref, gu_ref, gd_ref,
    gath, part, wu, wd, rs_out, rs_in, fin, y_out, y_in, slope_ref, ag, acc_up, acc_down,
    gi_sib_out, gi_sib_in, gi_out, gi_in,
    w_sem, gath_ss, gath_rs, sib_ss, sib_rs, rs_ss, rs_rs, y_ss, y_rs,
    agy_ss, agy_rs, ag_ss, ag_rs, gs_ss, gs_rs, gi_ss, gi_rs,
):
    r, c = lax.axis_index("row"), lax.axis_index("col")
    o, p = lax.div(r, 2), lax.rem(r, 2)
    z, yh = lax.div(c, 2), lax.rem(c, 2)
    along = ((r, lax.rem(c + 2, 16)), (r, lax.rem(c + 14, 16)))
    partner = (r, c + 1 - 2 * yh)
    sibling = (r + 1 - 2 * p, c)

    def peer(index):
        return (2 * index + p, c)

    def remote(src, dst, send, recv, device):
        return pltpu.make_async_remote_copy(
            src_ref=src, dst_ref=dst, send_sem=send, recv_sem=recv,
            device_id=device, device_id_type=MESH,
        )

    barrier = pltpu.get_barrier_semaphore()
    for device in along + (partner, sibling):
        pl.semaphore_signal(barrier, inc=1, device_id=device, device_id_type=MESH)
    for k in range(1, 8):
        pl.semaphore_signal(
            barrier, inc=1, device_id=peer(mod8(o + k)), device_id_type=MESH
        )
    w_copies = [
        pltpu.make_async_copy(wu_ref, wu, w_sem.at[0]),
        pltpu.make_async_copy(wd_ref, wd, w_sem.at[1]),
    ]
    for copy in w_copies:
        copy.start()
    gath[0, r] = x_ref[...]
    gath[1, r] = g_ref[...]
    pl.semaphore_wait(barrier, 11)

    def gather_copy(a, i):
        to = mod8(o - z - REL[i])
        return to, remote(
            gath.at[a, r], gath.at[a, r], gath_ss.at[a, i], gath_rs.at[a, o], peer(to)
        )

    def go(a, *which):
        for i in which:
            to, copy = gather_copy(a, i)

            @pl.when(to != o)
            def _(copy=copy):
                copy.start()

    def sibling_copy(a, i, parity):
        block = gath.at[a, 2 * mod8(o + z + REL[i]) + parity]
        return remote(block, block, sib_ss.at[a, i], sib_rs.at[a, i], sibling)

    def forward(a, *which):
        for i in which:
            source = mod8(o + z + REL[i])
            block = gath.at[a, 2 * source + p]

            @pl.when(source != o)
            def _(source=source, block=block, i=i):
                remote(
                    block, block, gath_ss.at[a, i], gath_rs.at[a, source], sibling
                ).wait_recv()

            sibling_copy(a, i, p).start()

    def tokens(a, *which):
        blocks = []
        for i in which:
            source = mod8(o + z + REL[i])
            blocks += [gath[a, 2 * source], gath[a, 2 * source + 1]]
        return jnp.concatenate(blocks, axis=0)

    def slots(t):
        return {0: (0,), 1: (1, 2), 2: (3, 4), 3: (5, 6), 4: (7,)}[t]

    def compute(a, t):
        for i in slots(t):
            sibling_copy(a, i, 1 - p).wait_recv()
        left = tokens(a, *slots(t))
        if a == 0:
            terms = dot(left, wu[...], 1, 0)
        else:
            terms = dot(left, wd[...], 1, 1)
        part[(t + a) % 2, pl.ds(0, 256 * len(slots(t))), :] = terms

    def ring_copy(a, t, d, j, h):
        at = (a, d, t, 2 * j + h)
        return remote(rs_out.at[at], rs_in.at[at], rs_ss.at[at], rs_rs.at[at], along[d])

    def chunk(a, t, d, j, h):
        rows = pl.ds((256 * d if t else 0) + 128 * j + HALF * h, HALF)
        total = part[(t + a) % 2, rows, :]
        if t > 1 or (t == 1 and h == d):
            ring_copy(a, t - 1, d, j, h).wait_recv()
            total += rs_in[a, d, t - 1, 2 * j + h].astype(F32)
        rs_out[a, d, t, 2 * j + h] = total.astype(BF)
        ring_copy(a, t, d, j, h).start()

    def first(a):
        for j in range(2):
            for d in range(2):
                chunk(a, 0, d, j, d)

    def group(a, t, j):
        for h in range(2):
            chunk(a, t, 0, j, h)
            chunk(a, t, 1, j, 1 - h)

    def last(a):
        for j, h in PARTS:
            rows = pl.ds(128 * j + HALF * h, HALF)
            total = part[a, rows, :]
            for d in range(2):
                ring_copy(a, 3, d, j, h).wait_recv()
                total += rs_in[a, d, 3, 2 * j + h].astype(F32)
            fin[a, rows, :] = total
            y_out[a, rows, :] = total.astype(BF)
        y_copy(a).start()

    def y_copy(a):
        return remote(
            y_out.at[a, pl.ds((1 - yh) * 128, 128)], y_in.at[a], y_ss.at[a], y_rs.at[a], partner
        )

    def reduced(a):
        y_copy(a).wait_recv()
        return fin[a, pl.ds(yh * 128, 128), :] + y_in[a].astype(F32)

    def agy_copy(a, j):
        block = ag.at[a, z, j]
        return remote(block, block, agy_ss.at[a], agy_rs.at[a], partner)

    def zed(d, t):
        return mod8(z - t) if d == 0 else mod8(z + t)

    def ag_copy(a, t, d, j, h, source):
        piece = ag.at[a, zed(d, source), j, pl.ds(h * HALF, HALF)]
        at = (a, d, t - 1, 2 * j + h)
        return remote(piece, piece, ag_ss.at[at], ag_rs.at[at], along[d])

    def ag_own(a, value):
        ag[a, z, yh] = value.astype(BF)
        agy_copy(a, yh).start()

    def ag_first(a):
        for j in (yh, 1 - yh):
            for h in range(2):
                for d in range(2):
                    ag_copy(a, 1, d, j, h, 0).start()
            if j is yh:
                agy_copy(a, 1 - yh).wait_recv()

    def ag_group(a, t, j):
        for h in range(2):
            for d in (h, 1 - h):
                if t < 4 or h == d:
                    ag_copy(a, t, d, j, h, t).wait_recv()
                if t < 3 or (t == 3 and h == d):
                    ag_copy(a, t + 1, d, j, h, t).start()

    def near(t):
        return {0: (7,), 1: (5, 6), 2: (3, 4), 3: (1, 2), 4: (0,)}[t]

    def gathered(a, t):
        blocks = []
        for i in near(t):
            source = mod8(z + REL[i])
            blocks += [ag[a, source, 0], ag[a, source, 1]]
        return jnp.concatenate(blocks, axis=0)

    def accumulate(acc, left, right, start):
        for m in range(3):
            rows = pl.ds(m * 256, 256)
            term = dot(left[:, m * 256 : (m + 1) * 256], right, 0, 0)
            if start:
                acc[rows, :] = term
            else:
                acc[rows, :] += term

    def add_down(t):
        accumulate(acc_down, gathered(0, t), tokens(1, *near(t)), t == 0)

    def add_up(t):
        accumulate(acc_up, tokens(0, *near(t)), gathered(1, t), t == 0)

    def gi_sib_copy(i):
        return remote(
            gi_sib_out.at[i], gi_sib_in.at[i], gs_ss.at[i], gs_rs.at[i], sibling
        )

    def gi_copy(i):
        return remote(
            gi_out.at[i], gi_in.at[o], gi_ss.at[i], gi_rs.at[o], peer(mod8(o + z + REL[i]))
        )

    def gi_start(t):
        part[t % 2, pl.ds(0, 256 * len(near(t))), :] = dot(gathered(1, t), wu[...], 1, 1)
        for n, i in enumerate(near(t)):
            rows = pl.ds(n * 256 + (1 - p) * 128, 128)
            gi_sib_out[i] = part[t % 2, rows, :].astype(BF)
            gi_sib_copy(i).start()

    def gi_finish(t):
        for n, i in enumerate(near(t)):
            gi_sib_copy(i).wait_recv()
            rows = pl.ds(n * 256 + p * 128, 128)
            total = (part[t % 2, rows, :] + gi_sib_in[i].astype(F32)).astype(BF)
            dest = mod8(o + z + REL[i])

            @pl.when(dest == o)
            def _(total=total):
                gi_in[o] = total

            @pl.when(dest != o)
            def _(total=total, i=i):
                gi_out[i] = total
                gi_copy(i).start()

    go(0, 0)
    forward(0, 0)
    go(0, 1, 2)
    w_copies[0].wait()
    compute(0, 0)
    first(0)
    forward(0, 1, 2)
    go(0, 3, 4)
    compute(0, 1)
    group(0, 1, 0)
    go(0, 5, 6)
    forward(0, 3, 4)
    group(0, 1, 1)
    compute(0, 2)
    group(0, 2, 0)
    go(0, 7)
    go(1, 0)
    forward(0, 5, 6)
    group(0, 2, 1)
    compute(0, 3)
    group(0, 3, 0)
    go(1, 1, 2)
    forward(0, 7)
    forward(1, 0)
    group(0, 3, 1)
    compute(0, 4)
    go(1, 3, 4)

    w_copies[1].wait()
    compute(1, 0)
    first(1)
    forward(1, 1, 2)
    last(0)
    compute(1, 1)
    group(1, 1, 0)
    go(1, 5, 6)
    forward(1, 3, 4)
    group(1, 1, 1)
    compute(1, 2)
    group(1, 2, 0)
    go(1, 7)
    forward(1, 5, 6)
    group(1, 2, 1)
    compute(1, 3)
    value, slope = gelu_parts(reduced(0))
    slope_ref[...] = slope
    ag_own(0, value)
    group(1, 3, 0)
    forward(1, 7)
    group(1, 3, 1)
    compute(1, 4)
    ag_first(0)
    last(1)

    add_down(0)
    ag_group(0, 1, 0)
    ag_group(0, 1, 1)
    ag_own(1, reduced(1) * slope_ref[...])
    add_down(1)
    ag_group(0, 2, 0)
    ag_group(0, 2, 1)
    add_down(2)
    ag_group(0, 3, 0)
    ag_group(0, 3, 1)
    ag_first(1)
    add_down(3)
    ag_group(0, 4, 0)
    ag_group(0, 4, 1)

    gi_start(0)
    add_up(0)
    gi_finish(0)
    ag_group(1, 1, 0)
    add_down(4)
    ag_group(1, 1, 1)
    gi_start(1)
    add_up(1)
    ag_group(1, 2, 0)
    gi_finish(1)
    ag_group(1, 2, 1)
    gi_start(2)
    add_up(2)
    ag_group(1, 3, 0)
    gi_finish(2)
    ag_group(1, 3, 1)
    gi_start(3)
    add_up(3)
    gi_finish(3)
    ag_group(1, 4, 0)
    ag_group(1, 4, 1)
    gi_start(4)
    add_up(4)
    gi_finish(4)
    factor = 1.0 / math.sqrt(2048)
    gd_ref[...] = (acc_down[...] * factor).astype(BF)
    gu_ref[...] = (acc_up[...] * factor).astype(BF)

    total = gi_in[o].astype(F32)
    for k in range(1, 8):
        source = mod8(o + k)
        remote(
            gi_out.at[0], gi_in.at[source], gi_ss.at[0], gi_rs.at[source], sibling
        ).wait_recv()
        total += gi_in[source].astype(F32)
    gi_ref[...] = total.astype(BF)

    for a in range(2):
        y_copy(a).wait_send()
        agy_copy(a, yh).wait_send()
        for i in range(8):
            to, copy = gather_copy(a, i)

            @pl.when(to != o)
            def _(copy=copy):
                copy.wait_send()

            sibling_copy(a, i, p).wait_send()
        for d in range(2):
            for j, h in PARTS:
                for t in range(4):
                    if t > 0 or h == d:
                        ring_copy(a, t, d, j, h).wait_send()
                    if t < 3 or h == d:
                        ag_copy(a, t + 1, d, j, h, t).wait_send()
    for i in range(8):
        gi_sib_copy(i).wait_send()

        @pl.when(mod8(o + z + REL[i]) != o)
        def _(i=i):
            gi_copy(i).wait_send()


def on_device(inputs, w_up, w_down, upstream):
    tokens, width = inputs.shape
    hidden = w_up.shape[1]
    dma = pltpu.SemaphoreType.DMA
    vmem = pl.BlockSpec(memory_space=pltpu.VMEM)
    anywhere = pl.BlockSpec(memory_space=pl.ANY)
    return pl.pallas_call(
        kernel,
        out_shape=(
            jax.ShapeDtypeStruct((tokens, width), BF),
            jax.ShapeDtypeStruct((width, hidden), BF),
            jax.ShapeDtypeStruct((hidden, width), BF),
        ),
        in_specs=[vmem, anywhere, anywhere, vmem],
        out_specs=(vmem, vmem, vmem),
        scratch_shapes=[
            pltpu.VMEM((2, 16, 128, 768), BF),
            pltpu.VMEM((2, 512, 768), F32),
            pltpu.VMEM((768, 768), BF),
            pltpu.VMEM((768, 768), BF),
            pltpu.VMEM((2, 2, 4, 4, HALF, 768), BF),
            pltpu.VMEM((2, 2, 4, 4, HALF, 768), BF),
            pltpu.VMEM((2, 256, 768), F32),
            pltpu.VMEM((2, 256, 768), BF),
            pltpu.VMEM((2, 128, 768), BF),
            pltpu.VMEM((128, 768), F32),
            pltpu.VMEM((2, 8, 2, 128, 768), BF),
            pltpu.VMEM((768, 768), F32),
            pltpu.VMEM((768, 768), F32),
            pltpu.VMEM((8, 128, 768), BF),
            pltpu.VMEM((8, 128, 768), BF),
            pltpu.VMEM((8, 128, 768), BF),
            pltpu.VMEM((8, 128, 768), BF),
            dma((2,)), dma((2, 8)), dma((2, 8)), dma((2, 8)), dma((2, 8)),
            dma((2, 2, 4, 4)), dma((2, 2, 4, 4)),
            dma((2,)), dma((2,)), dma((2,)), dma((2,)),
            dma((2, 2, 4, 4)), dma((2, 2, 4, 4)),
            dma((8,)), dma((8,)), dma((8,)), dma((8,)),
        ],
        compiler_params=pltpu.CompilerParams(
            collective_id=0, has_side_effects=True, vmem_limit_bytes=58 << 20
        ),
        cost_estimate=pl.CostEstimate(
            flops=5 * 2 * 2048 * 768 * 768, bytes_accessed=6 << 20, transcendentals=128 * 768
        ),
        name="block_backward",
    )(inputs, w_up, w_down, upstream)


def solution(mesh):
    in_specs = (P("row", "col"), P("col", "row"), P("row", "col"), P("row", "col"))
    out_specs = (P("row", "col"), P("col", "row"), P("row", "col"))
    return jax.shard_map(
        on_device, mesh=mesh, in_specs=in_specs, out_specs=out_specs, check_vma=False
    )
```

```python
import functools
import math

import jax
import jax.numpy as jnp
from jax import lax
from jax.experimental import pallas as pl
from jax.experimental.pallas import tpu as pltpu
from jax.sharding import PartitionSpec as P

MESH = pl.DeviceIdType.MESH
BF = jnp.bfloat16
F32 = jnp.float32
HALF = 64
REL = (4, 3, -3, 2, -2, 1, -1, 0)
PARTS = tuple((j, h) for j in range(2) for h in range(2))


def mod8(value):
    return lax.rem(value + 64, 8)


def gelu_parts(preact):
    coeff = math.sqrt(2.0 / math.pi)
    cubic = 0.044715
    inner = coeff * (preact + cubic * preact * preact * preact)
    tangent = jnp.tanh(inner)
    value = 0.5 * preact * (1.0 + tangent)
    slope = 0.5 * (1.0 + tangent) + 0.5 * preact * (1.0 - tangent * tangent) * coeff * (
        1.0 + 3.0 * cubic * preact * preact
    )
    return (value, slope)


def dot(left, right, left_dim, right_dim):
    return lax.dot_general(
        left, right, (((left_dim,), (right_dim,)), ((), ())), preferred_element_type=F32
    )


def kernel(
    x_ref, wu_ref, wd_ref, g_ref,
    gi_hbm, gu_hbm, gd_hbm,
    gi_ref, gu_ref, gd_ref, gath, part, wu, wd, rs_out, rs_in, fin, y_out, y_in, slope_ref, ag, acc_up, acc_down,
    gi_sib_out, gi_sib_in, gi_out, gi_in,
    out_sem, w_sem, gath_ss, gath_rs, sib_ss, sib_rs, rs_ss, rs_rs, y_ss, y_rs,
    agy_ss, agy_rs, ag_ss, ag_rs, gs_ss, gs_rs, gi_ss, gi_rs,
):
    r, c = lax.axis_index("row"), lax.axis_index("col")
    o, p = lax.div(r, 2), lax.rem(r, 2)
    z, yh = lax.div(c, 2), lax.rem(c, 2)
    along = ((r, lax.rem(c + 2, 16)), (r, lax.rem(c + 14, 16)))
    partner = (r, c + 1 - 2 * yh)
    sibling = (r + 1 - 2 * p, c)

    def peer(index):
        return (2 * index + p, c)

    def remote(src, dst, send, recv, device):
        return pltpu.make_async_remote_copy(
            src_ref=src, dst_ref=dst, send_sem=send, recv_sem=recv,
            device_id=device, device_id_type=MESH,
        )

    barrier = pltpu.get_barrier_semaphore()
    for device in along + (partner, sibling):
        pl.semaphore_signal(barrier, inc=1, device_id=device, device_id_type=MESH)
    for k in range(1, 8):
        pl.semaphore_signal(
            barrier, inc=1, device_id=peer(mod8(o + k)), device_id_type=MESH
        )
    w_copies = [
        pltpu.make_async_copy(wu_ref, wu, w_sem.at[0]),
        pltpu.make_async_copy(wd_ref, wd, w_sem.at[1]),
    ]
    for copy in w_copies:
        copy.start()
    gath[0, r] = x_ref[...]
    gath[1, r] = g_ref[...]
    pl.semaphore_wait(barrier, 11)

    def gather_copy(a, i):
        to = mod8(o - z - REL[i])
        return to, remote(
            gath.at[a, r], gath.at[a, r], gath_ss.at[a, i], gath_rs.at[a, o], peer(to)
        )

    def go(a, *which):
        for i in which:
            to, copy = gather_copy(a, i)

            @pl.when(to != o)
            def _(copy=copy):
                copy.start()

    def sibling_copy(a, i, parity):
        block = gath.at[a, 2 * mod8(o + z + REL[i]) + parity]
        return remote(block, block, sib_ss.at[a, i], sib_rs.at[a, i], sibling)

    def forward(a, *which):
        for i in which:
            source = mod8(o + z + REL[i])
            block = gath.at[a, 2 * source + p]

            @pl.when(source != o)
            def _(source=source, block=block, i=i):
                remote(
                    block, block, gath_ss.at[a, i], gath_rs.at[a, source], sibling
                ).wait_recv()

            sibling_copy(a, i, p).start()

    def tokens(a, *which):
        blocks = []
        for i in which:
            source = mod8(o + z + REL[i])
            blocks += [gath[a, 2 * source], gath[a, 2 * source + 1]]
        return jnp.concatenate(blocks, axis=0)

    def slots(t):
        return {0: (0,), 1: (1, 2), 2: (3, 4), 3: (5, 6), 4: (7,)}[t]

    def compute(a, t):
        for i in slots(t):
            sibling_copy(a, i, 1 - p).wait_recv()
        left = tokens(a, *slots(t))
        if a == 0:
            terms = dot(left, wu[...], 1, 0)
        else:
            terms = dot(left, wd[...], 1, 1)
        part[(t + a) % 2, pl.ds(0, 256 * len(slots(t))), :] = terms

    def ring_copy(a, t, d, j, h):
        at = (a, d, t, 2 * j + h)
        return remote(rs_out.at[at], rs_in.at[at], rs_ss.at[at], rs_rs.at[at], along[d])

    def chunk(a, t, d, j, h):
        rows = pl.ds((256 * d if t else 0) + 128 * j + HALF * h, HALF)
        total = part[(t + a) % 2, rows, :]
        if t > 1 or (t == 1 and h == d):
            ring_copy(a, t - 1, d, j, h).wait_recv()
            total += rs_in[a, d, t - 1, 2 * j + h].astype(F32)
        rs_out[a, d, t, 2 * j + h] = total.astype(BF)
        ring_copy(a, t, d, j, h).start()

    def first(a):
        for j in range(2):
            for d in range(2):
                chunk(a, 0, d, j, d)

    def group(a, t, j):
        for h in range(2):
            chunk(a, t, 0, j, h)
            chunk(a, t, 1, j, 1 - h)

    def last(a):
        for j, h in PARTS:
            rows = pl.ds(128 * j + HALF * h, HALF)
            total = part[a, rows, :]
            for d in range(2):
                ring_copy(a, 3, d, j, h).wait_recv()
                total += rs_in[a, d, 3, 2 * j + h].astype(F32)
            fin[a, rows, :] = total
            y_out[a, rows, :] = total.astype(BF)
        y_copy(a).start()

    def y_copy(a):
        return remote(
            y_out.at[a, pl.ds((1 - yh) * 128, 128)], y_in.at[a], y_ss.at[a], y_rs.at[a], partner
        )

    def reduced(a):
        y_copy(a).wait_recv()
        return fin[a, pl.ds(yh * 128, 128), :] + y_in[a].astype(F32)

    def agy_copy(a, j):
        block = ag.at[a, z, j]
        return remote(block, block, agy_ss.at[a], agy_rs.at[a], partner)

    def zed(d, t):
        return mod8(z - t) if d == 0 else mod8(z + t)

    def ag_copy(a, t, d, j, h, source):
        piece = ag.at[a, zed(d, source), j, pl.ds(h * HALF, HALF)]
        at = (a, d, t - 1, 2 * j + h)
        return remote(piece, piece, ag_ss.at[at], ag_rs.at[at], along[d])

    def ag_own(a, value):
        ag[a, z, yh] = value.astype(BF)
        agy_copy(a, yh).start()

    def ag_first(a, j):
        @pl.when(yh != j)
        def _():
            agy_copy(a, j).wait_recv()

        for h in range(2):
            for d in range(2):
                ag_copy(a, 1, d, j, h, 0).start()

    def ag_group(a, t, j):
        for h in range(2):
            for d in (h, 1 - h):
                if t < 4 or h == d:
                    ag_copy(a, t, d, j, h, t).wait_recv()
                if t < 3 or (t == 3 and h == d):
                    ag_copy(a, t + 1, d, j, h, t).start()

    def near(t):
        return {0: (7,), 1: (5, 6), 2: (3, 4), 3: (1, 2), 4: (0,)}[t]

    def gathered(a, t):
        blocks = []
        for i in near(t):
            source = mod8(z + REL[i])
            blocks += [ag[a, source, 0], ag[a, source, 1]]
        return jnp.concatenate(blocks, axis=0)

    def add_down(j, t):
        left = jnp.concatenate([ag[0, mod8(z + REL[i]), j] for i in near(t)], axis=0)
        right = jnp.concatenate(
            [gath[1, 2 * mod8(o + z + REL[i]) + j] for i in near(t)], axis=0
        )
        for m in range(3):
            rows = pl.ds(m * 256, 256)
            term = dot(left[:, m * 256 : (m + 1) * 256], right, 0, 0)
            if (j, t) == (0, 0):
                acc_down[rows, :] = term
            elif (j, t) != (1, 4):
                acc_down[rows, :] += term
            else:
                gd_ref[rows, :] = ((acc_down[rows, :] + term) * factor).astype(BF)
                out_copy(2 + m).start()

    def add_up(t):
        left, right = tokens(0, *near(t)), gathered(1, t)
        for m in range(3):
            rows = pl.ds(m * 256, 256)
            term = dot(left[:, m * 256 : (m + 1) * 256], right, 0, 0)
            if t == 0:
                acc_up[rows, :] = term
            else:
                acc_up[rows, :] += term

    def out_copy(n):
        if n == 0:
            return pltpu.make_async_copy(gi_ref, gi_hbm, out_sem.at[0])
        if n == 1:
            return pltpu.make_async_copy(gu_ref, gu_hbm, out_sem.at[1])
        rows = pl.ds((n - 2) * 256, 256)
        return pltpu.make_async_copy(gd_ref.at[rows], gd_hbm.at[rows], out_sem.at[n])

    def gi_sib_copy(i):
        return remote(
            gi_sib_out.at[i], gi_sib_in.at[i], gs_ss.at[i], gs_rs.at[i], sibling
        )

    def gi_copy(i):
        return remote(
            gi_out.at[i], gi_in.at[o], gi_ss.at[i], gi_rs.at[o], peer(mod8(o + z + REL[i]))
        )

    def gi_start(t):
        part[t % 2, pl.ds(0, 256 * len(near(t))), :] = dot(gathered(1, t), wu[...], 1, 1)
        for n, i in enumerate(near(t)):
            rows = pl.ds(n * 256 + (1 - p) * 128, 128)
            gi_sib_out[i] = part[t % 2, rows, :].astype(BF)
            gi_sib_copy(i).start()

    def gi_finish(t):
        for n, i in enumerate(near(t)):
            gi_sib_copy(i).wait_recv()
            rows = pl.ds(n * 256 + p * 128, 128)
            total = (part[t % 2, rows, :] + gi_sib_in[i].astype(F32)).astype(BF)
            dest = mod8(o + z + REL[i])

            @pl.when(dest == o)
            def _(total=total):
                gi_in[o] = total

            @pl.when(dest != o)
            def _(total=total, i=i):
                gi_out[i] = total
                gi_copy(i).start()

    go(0, 0)
    forward(0, 0)
    go(0, 1, 2)
    w_copies[0].wait()
    compute(0, 0)
    first(0)
    forward(0, 1, 2)
    go(0, 3, 4)
    compute(0, 1)
    group(0, 1, 0)
    go(0, 5, 6)
    forward(0, 3, 4)
    group(0, 1, 1)
    compute(0, 2)
    group(0, 2, 0)
    go(0, 7)
    go(1, 0)
    forward(0, 5, 6)
    group(0, 2, 1)
    compute(0, 3)
    group(0, 3, 0)
    go(1, 1, 2)
    forward(0, 7)
    forward(1, 0)
    group(0, 3, 1)
    compute(0, 4)
    go(1, 3, 4)

    w_copies[1].wait()
    compute(1, 0)
    first(1)
    forward(1, 1, 2)
    last(0)
    compute(1, 1)
    group(1, 1, 0)
    go(1, 5, 6)
    forward(1, 3, 4)
    group(1, 1, 1)
    compute(1, 2)
    group(1, 2, 0)
    go(1, 7)
    forward(1, 5, 6)
    group(1, 2, 1)
    compute(1, 3)
    value, slope = gelu_parts(reduced(0))
    slope_ref[...] = slope
    ag_own(0, value)
    group(1, 3, 0)
    forward(1, 7)
    group(1, 3, 1)
    compute(1, 4)
    ag_first(0, 0)
    last(1)

    factor = 1.0 / math.sqrt(2048)
    add_down(0, 0)
    ag_group(0, 1, 0)
    ag_own(1, reduced(1) * slope_ref[...])
    add_down(0, 1)
    ag_group(0, 2, 0)
    add_down(0, 2)
    ag_group(0, 3, 0)
    ag_first(1, 0)
    ag_first(1, 1)
    add_down(0, 3)
    ag_group(0, 4, 0)

    gi_start(0)
    add_up(0)
    gi_finish(0)
    ag_group(1, 1, 0)
    add_down(0, 4)
    ag_group(1, 1, 1)
    gi_start(1)
    add_up(1)
    ag_group(1, 2, 0)
    gi_finish(1)
    ag_group(1, 2, 1)
    gi_start(2)
    add_up(2)
    ag_group(1, 3, 0)
    gi_finish(2)
    ag_group(1, 3, 1)
    ag_first(0, 1)
    gi_start(3)
    add_up(3)
    gi_finish(3)
    ag_group(1, 4, 0)
    ag_group(1, 4, 1)
    gi_start(4)
    ag_group(0, 1, 1)
    gi_finish(4)
    add_up(4)

    gu_ref[...] = (acc_up[...] * factor).astype(BF)
    out_copy(1).start()
    add_down(1, 0)
    add_down(1, 1)
    ag_group(0, 2, 1)
    add_down(1, 2)
    ag_group(0, 3, 1)
    add_down(1, 3)
    total = gi_in[o].astype(F32)
    for k in range(1, 8):
        source = mod8(o + k)
        remote(
            gi_out.at[0], gi_in.at[source], gi_ss.at[0], gi_rs.at[source], sibling
        ).wait_recv()
        total += gi_in[source].astype(F32)
    gi_ref[...] = total.astype(BF)
    out_copy(0).start()
    ag_group(0, 4, 1)
    add_down(1, 4)

    for n in range(5):
        out_copy(n).wait()
    for a in range(2):
        y_copy(a).wait_send()
        agy_copy(a, yh).wait_send()
        for i in range(8):
            to, copy = gather_copy(a, i)

            @pl.when(to != o)
            def _(copy=copy):
                copy.wait_send()

            sibling_copy(a, i, p).wait_send()
        for d in range(2):
            for j, h in PARTS:
                for t in range(4):
                    if t > 0 or h == d:
                        ring_copy(a, t, d, j, h).wait_send()
                    if t < 3 or h == d:
                        ag_copy(a, t + 1, d, j, h, t).wait_send()
    for i in range(8):
        gi_sib_copy(i).wait_send()

        @pl.when(mod8(o + z + REL[i]) != o)
        def _(i=i):
            gi_copy(i).wait_send()


def copy_kernel(*refs):
    sources, targets, stages, sem = refs[:3], refs[3:6], refs[6:9], refs[9]
    pieces = [(0, 0, 128)] + [(n, m * 256, 256) for n in (1, 2) for m in range(3)]

    def copies(k):
        n, start, extent = pieces[k]
        rows = pl.ds(start, extent)
        return (
            pltpu.make_async_copy(sources[n].at[rows], stages[n].at[rows], sem.at[0, k]),
            pltpu.make_async_copy(stages[n].at[rows], targets[n].at[rows], sem.at[1, k]),
        )

    for k in range(len(pieces)):
        copies(k)[0].start()
    for k in range(len(pieces)):
        copies(k)[0].wait()
        copies(k)[1].start()
    for k in range(len(pieces)):
        copies(k)[1].wait()


def on_device(*args):
    results = block(*args)
    anywhere = pl.BlockSpec(memory_space=pl.ANY)
    return pl.pallas_call(
        copy_kernel,
        out_shape=tuple(jax.ShapeDtypeStruct(t.shape, t.dtype) for t in results),
        in_specs=[anywhere] * 3,
        out_specs=(anywhere,) * 3,
        scratch_shapes=[pltpu.VMEM(t.shape, t.dtype) for t in results]
        + [pltpu.SemaphoreType.DMA((2, 7))],
        compiler_params=pltpu.CompilerParams(vmem_limit_bytes=58 << 20),
        name="hand_over",
    )(*results)


def block(inputs, w_up, w_down, upstream):
    tokens, width = inputs.shape
    hidden = w_up.shape[1]
    dma = pltpu.SemaphoreType.DMA
    vmem = pl.BlockSpec(memory_space=pltpu.VMEM)
    anywhere = pl.BlockSpec(memory_space=pl.ANY)
    return pl.pallas_call(
        kernel,
        out_shape=(
            jax.ShapeDtypeStruct((tokens, width), BF),
            jax.ShapeDtypeStruct((width, hidden), BF),
            jax.ShapeDtypeStruct((hidden, width), BF),
        ),
        in_specs=[vmem, anywhere, anywhere, vmem],
        out_specs=(anywhere, anywhere, anywhere),
        scratch_shapes=[
            pltpu.VMEM((tokens, width), BF),
            pltpu.VMEM((width, hidden), BF),
            pltpu.VMEM((hidden, width), BF),
            pltpu.VMEM((2, 16, 128, 768), BF),
            pltpu.VMEM((2, 512, 768), F32),
            pltpu.VMEM((768, 768), BF),
            pltpu.VMEM((768, 768), BF),
            pltpu.VMEM((2, 2, 4, 4, HALF, 768), BF),
            pltpu.VMEM((2, 2, 4, 4, HALF, 768), BF),
            pltpu.VMEM((2, 256, 768), F32),
            pltpu.VMEM((2, 256, 768), BF),
            pltpu.VMEM((2, 128, 768), BF),
            pltpu.VMEM((128, 768), F32),
            pltpu.VMEM((2, 8, 2, 128, 768), BF),
            pltpu.VMEM((768, 768), F32),
            pltpu.VMEM((768, 768), F32),
            pltpu.VMEM((8, 128, 768), BF),
            pltpu.VMEM((8, 128, 768), BF),
            pltpu.VMEM((8, 128, 768), BF),
            pltpu.VMEM((8, 128, 768), BF),
            dma((5,)), dma((2,)), dma((2, 8)), dma((2, 8)), dma((2, 8)), dma((2, 8)),
            dma((2, 2, 4, 4)), dma((2, 2, 4, 4)),
            dma((2,)), dma((2,)), dma((2,)), dma((2,)),
            dma((2, 2, 4, 4)), dma((2, 2, 4, 4)),
            dma((8,)), dma((8,)), dma((8,)), dma((8,)),
        ],
        compiler_params=pltpu.CompilerParams(
            collective_id=0, has_side_effects=True, vmem_limit_bytes=58 << 20
        ),
        cost_estimate=pl.CostEstimate(
            flops=5 * 2 * 2048 * 768 * 768, bytes_accessed=6 << 20, transcendentals=128 * 768
        ),
        name="block_backward",
    )(inputs, w_up, w_down, upstream)


def solution(mesh):
    in_specs = (P("row", "col"), P("col", "row"), P("row", "col"), P("row", "col"))
    out_specs = (P("row", "col"), P("col", "row"), P("row", "col"))
    return jax.shard_map(
        on_device, mesh=mesh, in_specs=in_specs, out_specs=out_specs, check_vma=False
    )
```

```python
import functools
import math

import jax
import jax.numpy as jnp
from jax import lax
from jax.experimental import pallas as pl
from jax.experimental.pallas import tpu as pltpu
from jax.sharding import PartitionSpec as P

MESH = pl.DeviceIdType.MESH
BF = jnp.bfloat16
F32 = jnp.float32
HALF = 64
REL = (4, 3, -3, 2, -2, 1, -1, 0)
PARTS = tuple((j, h) for j in range(2) for h in range(2))


def mod8(value):
    return lax.rem(value + 64, 8)


def gelu_parts(preact):
    coeff = math.sqrt(2.0 / math.pi)
    cubic = 0.044715
    inner = coeff * (preact + cubic * preact * preact * preact)
    tangent = jnp.tanh(inner)
    value = 0.5 * preact * (1.0 + tangent)
    slope = 0.5 * (1.0 + tangent) + 0.5 * preact * (1.0 - tangent * tangent) * coeff * (
        1.0 + 3.0 * cubic * preact * preact
    )
    return (value, slope)


def dot(left, right, left_dim, right_dim):
    return lax.dot_general(
        left, right, (((left_dim,), (right_dim,)), ((), ())), preferred_element_type=F32
    )


def kernel(
    x_ref, wu_ref, wd_ref, g_ref,
    gi_hbm, gu_hbm, gd_hbm,
    gi_ref, gu_ref, gd_ref, gath, part, wu, wd, rs_out, rs_in, fin, y_out, y_in, slope_ref, ag, acc_up, acc_down,
    gi_sib_out, gi_sib_in, gi_out, gi_in,
    out_sem, w_sem, gath_ss, gath_rs, sib_ss, sib_rs, rs_ss, rs_rs, y_ss, y_rs,
    agy_ss, agy_rs, ag_ss, ag_rs, gs_ss, gs_rs, gi_ss, gi_rs,
):
    r, c = lax.axis_index("row"), lax.axis_index("col")
    o, p = lax.div(r, 2), lax.rem(r, 2)
    z, yh = lax.div(c, 2), lax.rem(c, 2)
    along = ((r, lax.rem(c + 2, 16)), (r, lax.rem(c + 14, 16)))
    partner = (r, c + 1 - 2 * yh)
    sibling = (r + 1 - 2 * p, c)

    def peer(index):
        return (2 * index + p, c)

    def remote(src, dst, send, recv, device):
        return pltpu.make_async_remote_copy(
            src_ref=src, dst_ref=dst, send_sem=send, recv_sem=recv,
            device_id=device, device_id_type=MESH,
        )

    barrier = pltpu.get_barrier_semaphore()
    for device in along + (partner, sibling):
        pl.semaphore_signal(barrier, inc=1, device_id=device, device_id_type=MESH)
    for k in range(1, 8):
        pl.semaphore_signal(
            barrier, inc=1, device_id=peer(mod8(o + k)), device_id_type=MESH
        )
    w_copies = [
        pltpu.make_async_copy(wu_ref, wu, w_sem.at[0]),
        pltpu.make_async_copy(wd_ref, wd, w_sem.at[1]),
    ]
    for copy in w_copies:
        copy.start()
    gath[0, r] = x_ref[...]
    gath[1, r] = g_ref[...]
    pl.semaphore_wait(barrier, 11)

    def gather_copy(a, i):
        to = mod8(o - z - REL[i])
        return to, remote(
            gath.at[a, r], gath.at[a, r], gath_ss.at[a, i], gath_rs.at[a, o], peer(to)
        )

    def go(a, *which):
        for i in which:
            to, copy = gather_copy(a, i)

            @pl.when(to != o)
            def _(copy=copy):
                copy.start()

    def sibling_copy(a, i, parity):
        block = gath.at[a, 2 * mod8(o + z + REL[i]) + parity]
        return remote(block, block, sib_ss.at[a, i], sib_rs.at[a, i], sibling)

    def forward(a, *which):
        for i in which:
            source = mod8(o + z + REL[i])
            block = gath.at[a, 2 * source + p]

            @pl.when(source != o)
            def _(source=source, block=block, i=i):
                remote(
                    block, block, gath_ss.at[a, i], gath_rs.at[a, source], sibling
                ).wait_recv()

            sibling_copy(a, i, p).start()

    def tokens(a, *which):
        blocks = []
        for i in which:
            source = mod8(o + z + REL[i])
            blocks += [gath[a, 2 * source], gath[a, 2 * source + 1]]
        return jnp.concatenate(blocks, axis=0)

    def slots(t):
        return {0: (0,), 1: (1, 2), 2: (3, 4), 3: (5, 6), 4: (7,)}[t]

    def compute(a, t):
        for i in slots(t):
            sibling_copy(a, i, 1 - p).wait_recv()
        left = tokens(a, *slots(t))
        if a == 0:
            terms = dot(left, wu[...], 1, 0)
        else:
            terms = dot(left, wd[...], 1, 1)
        part[(t + a) % 2, pl.ds(0, 256 * len(slots(t))), :] = terms

    def ring_copy(a, t, d, j, h):
        at = (a, d, t, 2 * j + h)
        return remote(rs_out.at[at], rs_in.at[at], rs_ss.at[at], rs_rs.at[at], along[d])

    def chunk(a, t, d, j, h):
        rows = pl.ds((256 * d if t else 0) + 128 * j + HALF * h, HALF)
        total = part[(t + a) % 2, rows, :]
        if t > 1 or (t == 1 and h == d):
            ring_copy(a, t - 1, d, j, h).wait_recv()
            total += rs_in[a, d, t - 1, 2 * j + h].astype(F32)
        rs_out[a, d, t, 2 * j + h] = total.astype(BF)
        ring_copy(a, t, d, j, h).start()

    def first(a):
        for j in range(2):
            for d in range(2):
                chunk(a, 0, d, j, d)

    def group(a, t, j):
        for h in range(2):
            chunk(a, t, 0, j, h)
            chunk(a, t, 1, j, 1 - h)

    def last(a):
        for h in range(2):
            for j in range(2):
                rows = pl.ds(128 * j + HALF * h, HALF)
                total = part[a, rows, :]
                for d in range(2):
                    ring_copy(a, 3, d, j, h).wait_recv()
                    total += rs_in[a, d, 3, 2 * j + h].astype(F32)
                fin[a, rows, :] = total
                y_out[a, rows, :] = total.astype(BF)
            y_copy(a, h).start()

    def y_copy(a, h):
        return remote(
            y_out.at[a, pl.ds((1 - yh) * 128 + HALF * h, HALF)],
            y_in.at[a, pl.ds(HALF * h, HALF)], y_ss.at[a, h], y_rs.at[a, h], partner,
        )

    def reduced(a, h):
        y_copy(a, h).wait_recv()
        own = fin[a, pl.ds(yh * 128 + HALF * h, HALF), :]
        return own + y_in[a, pl.ds(HALF * h, HALF), :].astype(F32)

    def agy_copy(a, j, h):
        piece = ag.at[a, z, j, pl.ds(HALF * h, HALF)]
        return remote(piece, piece, agy_ss.at[a, h], agy_rs.at[a, h], partner)

    def zed(d, t):
        return mod8(z - t) if d == 0 else mod8(z + t)

    def ag_copy(a, t, d, j, h, source):
        piece = ag.at[a, zed(d, source), j, pl.ds(h * HALF, HALF)]
        at = (a, d, t - 1, 2 * j + h)
        return remote(piece, piece, ag_ss.at[at], ag_rs.at[at], along[d])

    def ag_own(a, h, value):
        ag[a, z, yh, pl.ds(HALF * h, HALF), :] = value.astype(BF)
        agy_copy(a, yh, h).start()

    def ag_first(a, j):
        for h in range(2):
            if a == 1:
                agy_copy(1, j, h).wait_recv()
            else:

                @pl.when(yh != j)
                def _(h=h):
                    agy_copy(0, j, h).wait_recv()

            ag_begin(a, j, h)

    def ag_begin(a, j, h):
        for d in range(2):
            ag_copy(a, 1, d, j, h, 0).start()

    def ag_group(a, t, j):
        for h in range(2):
            for d in (h, 1 - h):
                if t < 4 or h == d:
                    ag_copy(a, t, d, j, h, t).wait_recv()
                if t < 3 or (t == 3 and h == d):
                    ag_copy(a, t + 1, d, j, h, t).start()

    def near(t):
        return {0: (7,), 1: (5, 6), 2: (3, 4), 3: (1, 2), 4: (0,)}[t]

    def gathered(a, t):
        blocks = []
        for i in near(t):
            source = mod8(z + REL[i])
            blocks += [ag[a, source, 0], ag[a, source, 1]]
        return jnp.concatenate(blocks, axis=0)

    def add_down(j, t):
        left = jnp.concatenate([ag[0, mod8(z + REL[i]), j] for i in near(t)], axis=0)
        right = jnp.concatenate(
            [gath[1, 2 * mod8(o + z + REL[i]) + j] for i in near(t)], axis=0
        )
        for m in range(3):
            rows = pl.ds(m * 256, 256)
            term = dot(left[:, m * 256 : (m + 1) * 256], right, 0, 0)
            if (j, t) == (0, 0):
                acc_down[rows, :] = term
            elif (j, t) != (1, 4):
                acc_down[rows, :] += term
            else:
                gd_ref[rows, :] = ((acc_down[rows, :] + term) * factor).astype(BF)
                out_copy(2 + m).start()

    def add_up(t):
        left, right = tokens(0, *near(t)), gathered(1, t)
        for m in range(3):
            rows = pl.ds(m * 256, 256)
            term = dot(left[:, m * 256 : (m + 1) * 256], right, 0, 0)
            if t == 0:
                acc_up[rows, :] = term
            else:
                acc_up[rows, :] += term

    def out_copy(n):
        if n == 0:
            return pltpu.make_async_copy(gi_ref, gi_hbm, out_sem.at[0])
        if n == 1:
            return pltpu.make_async_copy(gu_ref, gu_hbm, out_sem.at[1])
        rows = pl.ds((n - 2) * 256, 256)
        return pltpu.make_async_copy(gd_ref.at[rows], gd_hbm.at[rows], out_sem.at[n])

    def gi_sib_copy(i):
        return remote(
            gi_sib_out.at[i], gi_sib_in.at[i], gs_ss.at[i], gs_rs.at[i], sibling
        )

    def gi_copy(i):
        return remote(
            gi_out.at[i], gi_in.at[o], gi_ss.at[i], gi_rs.at[o], peer(mod8(o + z + REL[i]))
        )

    def gi_start(t):
        part[t % 2, pl.ds(0, 256 * len(near(t))), :] = dot(gathered(1, t), wu[...], 1, 1)
        for n, i in enumerate(near(t)):
            rows = pl.ds(n * 256 + (1 - p) * 128, 128)
            gi_sib_out[i] = part[t % 2, rows, :].astype(BF)
            gi_sib_copy(i).start()

    def gi_finish(t):
        for n, i in enumerate(near(t)):
            gi_sib_copy(i).wait_recv()
            rows = pl.ds(n * 256 + p * 128, 128)
            total = (part[t % 2, rows, :] + gi_sib_in[i].astype(F32)).astype(BF)
            dest = mod8(o + z + REL[i])

            @pl.when(dest == o)
            def _(total=total):
                gi_in[o] = total

            @pl.when(dest != o)
            def _(total=total, i=i):
                gi_out[i] = total
                gi_copy(i).start()

    go(0, 0, 1, 2)
    forward(0, 0)
    w_copies[0].wait()
    compute(0, 0)
    first(0)
    go(0, 3, 4)
    forward(0, 1, 2)
    go(0, 5, 6)
    compute(0, 1)
    group(0, 1, 0)
    forward(0, 3, 4)
    go(0, 7)
    group(0, 1, 1)
    compute(0, 2)
    go(1, 0)
    group(0, 2, 0)
    forward(0, 5, 6)
    go(1, 1, 2)
    group(0, 2, 1)
    compute(0, 3)
    forward(0, 7)
    group(0, 3, 0)
    forward(1, 0)
    go(1, 3, 4)
    group(0, 3, 1)
    compute(0, 4)

    w_copies[1].wait()
    compute(1, 0)
    first(1)
    forward(1, 1, 2)
    go(1, 5, 6)
    last(0)
    compute(1, 1)
    group(1, 1, 0)
    forward(1, 3, 4)
    go(1, 7)
    group(1, 1, 1)
    compute(1, 2)
    group(1, 2, 0)
    forward(1, 5, 6)
    group(1, 2, 1)
    compute(1, 3)
    for h in range(2):
        value, slope = gelu_parts(reduced(0, h))
        slope_ref[pl.ds(HALF * h, HALF), :] = slope
        ag_own(0, h, value)
    group(1, 3, 0)
    forward(1, 7)
    group(1, 3, 1)
    compute(1, 4)
    ag_first(0, 0)
    last(1)

    factor = 1.0 / math.sqrt(2048)
    add_down(0, 0)
    ag_group(0, 1, 0)
    for h in range(2):
        ag_own(1, h, reduced(1, h) * slope_ref[pl.ds(HALF * h, HALF), :])
    add_down(0, 1)
    ag_group(0, 2, 0)
    for h in range(2):
        ag_begin(1, yh, h)
    add_down(0, 2)
    ag_group(0, 3, 0)
    ag_first(1, 1 - yh)
    add_down(0, 3)
    ag_group(0, 4, 0)

    gi_start(0)
    add_up(0)
    gi_finish(0)
    ag_group(1, 1, 0)
    add_down(0, 4)
    ag_group(1, 1, 1)
    gi_start(1)
    add_up(1)
    gi_finish(1)
    ag_group(1, 2, 0)
    ag_group(1, 2, 1)
    gi_start(2)
    add_up(2)
    gi_finish(2)
    ag_group(1, 3, 0)
    ag_group(1, 3, 1)
    ag_first(0, 1)
    gi_start(3)
    add_up(3)
    gi_finish(3)
    ag_group(1, 4, 0)
    ag_group(1, 4, 1)
    gi_start(4)
    ag_group(0, 1, 1)
    gi_finish(4)
    add_up(4)

    gu_ref[...] = (acc_up[...] * factor).astype(BF)
    out_copy(1).start()
    add_down(1, 0)
    add_down(1, 1)
    ag_group(0, 2, 1)
    add_down(1, 2)
    ag_group(0, 3, 1)
    add_down(1, 3)
    ag_group(0, 4, 1)
    add_down(1, 4)
    total = gi_in[o].astype(F32)
    for k in range(1, 8):
        source = mod8(o + k)
        remote(
            gi_out.at[0], gi_in.at[source], gi_ss.at[0], gi_rs.at[source], sibling
        ).wait_recv()
        total += gi_in[source].astype(F32)
    gi_ref[...] = total.astype(BF)
    out_copy(0).start()

    for n in range(5):
        out_copy(n).wait()
    for a in range(2):
        for h in range(2):
            y_copy(a, h).wait_send()
            agy_copy(a, yh, h).wait_send()
        for i in range(8):
            to, copy = gather_copy(a, i)

            @pl.when(to != o)
            def _(copy=copy):
                copy.wait_send()

            sibling_copy(a, i, p).wait_send()
        for d in range(2):
            for j, h in PARTS:
                for t in range(4):
                    if t > 0 or h == d:
                        ring_copy(a, t, d, j, h).wait_send()
                    if t < 3 or h == d:
                        ag_copy(a, t + 1, d, j, h, t).wait_send()
    for i in range(8):
        gi_sib_copy(i).wait_send()

        @pl.when(mod8(o + z + REL[i]) != o)
        def _(i=i):
            gi_copy(i).wait_send()


def copy_kernel(*refs):
    sources, targets, stages, sem = refs[:3], refs[3:6], refs[6:9], refs[9]
    pieces = [(0, 0, 128)] + [(n, m * 256, 256) for n in (1, 2) for m in range(3)]

    def copies(k):
        n, start, extent = pieces[k]
        rows = pl.ds(start, extent)
        return (
            pltpu.make_async_copy(sources[n].at[rows], stages[n].at[rows], sem.at[0, k]),
            pltpu.make_async_copy(stages[n].at[rows], targets[n].at[rows], sem.at[1, k]),
        )

    for k in range(len(pieces)):
        copies(k)[0].start()
    for k in range(len(pieces)):
        copies(k)[0].wait()
        copies(k)[1].start()
    for k in range(len(pieces)):
        copies(k)[1].wait()


def on_device(*args):
    results = block(*args)
    anywhere = pl.BlockSpec(memory_space=pl.ANY)
    return pl.pallas_call(
        copy_kernel,
        out_shape=tuple(jax.ShapeDtypeStruct(t.shape, t.dtype) for t in results),
        in_specs=[anywhere] * 3,
        out_specs=(anywhere,) * 3,
        scratch_shapes=[pltpu.VMEM(t.shape, t.dtype) for t in results]
        + [pltpu.SemaphoreType.DMA((2, 7))],
        compiler_params=pltpu.CompilerParams(vmem_limit_bytes=58 << 20),
        name="hand_over",
    )(*results)


def block(inputs, w_up, w_down, upstream):
    tokens, width = inputs.shape
    hidden = w_up.shape[1]
    dma = pltpu.SemaphoreType.DMA
    vmem = pl.BlockSpec(memory_space=pltpu.VMEM)
    anywhere = pl.BlockSpec(memory_space=pl.ANY)
    return pl.pallas_call(
        kernel,
        out_shape=(
            jax.ShapeDtypeStruct((tokens, width), BF),
            jax.ShapeDtypeStruct((width, hidden), BF),
            jax.ShapeDtypeStruct((hidden, width), BF),
        ),
        in_specs=[vmem, anywhere, anywhere, vmem],
        out_specs=(anywhere, anywhere, anywhere),
        scratch_shapes=[
            pltpu.VMEM((tokens, width), BF),
            pltpu.VMEM((width, hidden), BF),
            pltpu.VMEM((hidden, width), BF),
            pltpu.VMEM((2, 16, 128, 768), BF),
            pltpu.VMEM((2, 512, 768), F32),
            pltpu.VMEM((768, 768), BF),
            pltpu.VMEM((768, 768), BF),
            pltpu.VMEM((2, 2, 4, 4, HALF, 768), BF),
            pltpu.VMEM((2, 2, 4, 4, HALF, 768), BF),
            pltpu.VMEM((2, 256, 768), F32),
            pltpu.VMEM((2, 256, 768), BF),
            pltpu.VMEM((2, 128, 768), BF),
            pltpu.VMEM((128, 768), F32),
            pltpu.VMEM((2, 8, 2, 128, 768), BF),
            pltpu.VMEM((768, 768), F32),
            pltpu.VMEM((768, 768), F32),
            pltpu.VMEM((8, 128, 768), BF),
            pltpu.VMEM((8, 128, 768), BF),
            pltpu.VMEM((8, 128, 768), BF),
            pltpu.VMEM((8, 128, 768), BF),
            dma((5,)), dma((2,)), dma((2, 8)), dma((2, 8)), dma((2, 8)), dma((2, 8)),
            dma((2, 2, 4, 4)), dma((2, 2, 4, 4)),
            dma((2, 2)), dma((2, 2)), dma((2, 2)), dma((2, 2)),
            dma((2, 2, 4, 4)), dma((2, 2, 4, 4)),
            dma((8,)), dma((8,)), dma((8,)), dma((8,)),
        ],
        compiler_params=pltpu.CompilerParams(
            collective_id=0, has_side_effects=True, vmem_limit_bytes=58 << 20
        ),
        cost_estimate=pl.CostEstimate(
            flops=5 * 2 * 2048 * 768 * 768, bytes_accessed=6 << 20, transcendentals=128 * 768
        ),
        name="block_backward",
    )(inputs, w_up, w_down, upstream)


def solution(mesh):
    in_specs = (P("row", "col"), P("col", "row"), P("row", "col"), P("row", "col"))
    out_specs = (P("row", "col"), P("col", "row"), P("row", "col"))
    return jax.shard_map(
        on_device, mesh=mesh, in_specs=in_specs, out_specs=out_specs, check_vma=False
    )
```
